128 devices in a mesh: section: 2 (over z_hi), dp: 16 (over y, x), tp: 4 (over z_lo, core).
Axes of the slice: x: 4, y: 4, z: 4 (z_hi: 2, z_lo: 2; z = z_hi * 2 + z_lo), core: 2. Of those that a mesh axis runs over, the one named last changes fastest.
Arguments:
- tokens: bfloat16 [2, 8192, 1024], P(None, ('dp', 'tp')), may hold values from -6 to 6
- segments: int32 [2, 8192], P(None, 'dp'), may hold values from 0 to 2, as said below
- cotangent: bfloat16 [2, 8192, 1024], P(None, ('dp', 'tp')), may hold values from -6 to 6
- norm_gain: bfloat16 [2, 1024], P('section'), may hold values from 0.099609375 to 1.8984375
- gate_weight: bfloat16 [2, 1024, 2048], P('section', 'dp', 'tp'), may hold values from -0.1875 to 0.1875
- value_weight: bfloat16 [2, 1024, 2048], P('section', 'dp', 'tp'), may hold values from -0.1875 to 0.1875
- step_weight: bfloat16 [2, 1024, 32], P('section', 'dp', 'tp'), may hold values from -0.1875 to 0.1875
- state_weight: bfloat16 [2, 1024, 256], P('section', 'dp'), may hold values from -0.1875 to 0.1875
- conv_kernel: float32 [2, 4, 2048], P('section', None, 'tp'), may hold values from -3 to 3
- conv_offset: float32 [2, 2048], P('section', 'tp'), may hold values from -1.5 to 1.5
- state_kernel: float32 [2, 4, 256], P('section'), may hold values from -3 to 3
- state_offset: float32 [2, 256], P('section'), may hold values from -1.5 to 1.5
- decay_log: float32 [2, 32], P('section', 'tp'), may hold values from 0 to 2.77
- step_bias: float32 [2, 32], P('section', 'tp'), may hold values from -5 to -1
- skip_gain: float32 [2, 32], P('section', 'tp'), may hold values from 0.5 to 1.5
- mixer_gain: bfloat16 [2, 2048], P('section', 'tp'), may hold values from 0.099609375 to 1.8984375
- output_weight: bfloat16 [2, 2048, 1024], P('section', 'tp', 'dp'), may hold values from -0.125 to 0.125
Outputs:
- section_outputs: float32 [2, 2, 8192, 1024], P('section', None, ('dp', 'tp'))
- input_grads: float32 [2, 2, 8192, 1024], P('section', None, ('dp', 'tp'))
- grad_norm_gain: float32 [2, 1024], P('section', ('dp', 'tp'))
- grad_gate_weight: float32 [2, 1024, 2048], P('section', 'dp', 'tp')
- grad_value_weight: float32 [2, 1024, 2048], P('section', 'dp', 'tp')
- grad_step_weight: float32 [2, 1024, 32], P('section', 'dp', 'tp')
- grad_state_weight: float32 [2, 1024, 256], P('section', ('dp', 'tp'))
- grad_conv_kernel: float32 [2, 4, 2048], P('section', None, 'tp')
- grad_conv_offset: float32 [2, 2048], P('section', 'tp')
- grad_state_kernel: float32 [2, 4, 256], P('section', None, ('dp', 'tp'))
- grad_state_offset: float32 [2, 256], P('section', ('dp', 'tp'))
- grad_decay_log: float32 [2, 32], P('section', 'tp')
- grad_step_bias: float32 [2, 32], P('section', 'tp')
- grad_skip_gain: float32 [2, 32], P('section', 'tp')
- grad_mixer_gain: float32 [2, 2048], P('section', 'tp')
- grad_output_weight: float32 [2, 2048, 1024], P('section', 'tp', 'dp')
The draws below stay inside these ranges and needn't reach their ends.
Inputs may be any that keep to these rules, and one draw needn't show every extreme that they name: `segments`: within every row of 512 tokens the numbers start at 0, never fall, and rise by one at exactly two positions: one among positions 1 to 64, one among the last 64 positions.
All inputs are finite; a program needn't handle non-finite values.
Results may differ from the reference program's by a relative error of at most 0.018.
Values may be sent and summed in bfloat16 or wider, within the bound.
A program may use at most 192 MiB of HBM per device.

```python
import jax
import jax.numpy as jnp
from jax import lax

D = 1024
H = 32
N = 128
KC = 4
CH = 256
DI = 2048
ROW = 512
MICRO = 2
TOKENS = 8192
N_SECTION = 2


def draw_segments(key, part):
    key = jax.random.fold_in(key, 11)
    first_key, second_key = jax.random.split(key)
    row_total = TOKENS // ROW
    first_cut = jax.random.randint(first_key, (MICRO, row_total, 1), 1, ROW // 8 + 1)
    second_cut = jax.random.randint(second_key, (MICRO, row_total, 1), ROW - ROW // 8, ROW)
    places = jnp.arange(ROW, dtype=jnp.int32)[None, None, :]
    numbers = (places >= first_cut).astype(jnp.int32) + (places >= second_cut).astype(jnp.int32)
    return numbers.reshape(MICRO, TOKENS)


def levels(own_key, dims, shards, least, top_value):
    def one(position, shards_of):
        steps = jax.random.uniform(jax.random.fold_in(jax.random.fold_in(own_key, 6), position), (shards_of,), jnp.float32, least / len(shards), top_value / len(shards))
        return jnp.repeat(jnp.exp(steps), dims[position] // shards_of).reshape((-1,) + (1,) * (len(dims) - position - 1))

    gain = one(*shards[0])
    for cut in shards[1:]:
        gain = gain * one(*cut)
    return gain


def noise(key, dims, spread, most, cuts=(), kind=jnp.bfloat16):
    result = spread * jax.random.normal(key, dims, jnp.float32)
    if cuts:
        result = result * levels(key, dims, cuts, -0.22, 0.18)
    return jnp.clip(result, -most, most).astype(kind)


def setup_inputs(seed: int = 0) -> dict:
    streams_of = jax.random.split(jax.random.key(seed), 18)
    return {
        "tokens": noise(streams_of[0], (MICRO, TOKENS, D), 1.0, 6.0, ((1, 64),)),
        "segments": draw_segments(jax.random.fold_in(streams_of[17], 71), 0),
        "cotangent": noise(streams_of[2], (MICRO, TOKENS, D), 1.0, 6.0, ((1, 64),)),
        "norm_gain": jnp.clip(1.0 + 0.18 * jax.random.normal(streams_of[3], (N_SECTION, D), jnp.float32), 0.099609375, 1.8984375).astype(jnp.bfloat16),
        "gate_weight": noise(streams_of[4], (N_SECTION, D, DI), D ** -0.5, 0.1875, ((0, 2), (1, 16), (2, 4))),
        "value_weight": noise(streams_of[5], (N_SECTION, D, DI), D ** -0.5, 0.1875, ((0, 2), (1, 16), (2, 4))),
        "step_weight": noise(streams_of[6], (N_SECTION, D, H), D ** -0.5, 0.1875, ((0, 2), (1, 16), (2, 4))),
        "state_weight": noise(streams_of[7], (N_SECTION, D, 2 * N), D ** -0.5, 0.1875, ((0, 2), (1, 16))),
        "conv_kernel": noise(streams_of[8], (N_SECTION, KC, DI), KC ** -0.5, 3.0, ((0, 2), (2, 4)), jnp.float32),
        "conv_offset": noise(streams_of[9], (N_SECTION, DI), 0.3, 1.5, ((0, 2), (1, 4)), jnp.float32),
        "state_kernel": noise(streams_of[10], (N_SECTION, KC, 2 * N), KC ** -0.5, 3.0, ((0, 2),), jnp.float32),
        "state_offset": noise(streams_of[11], (N_SECTION, 2 * N), 0.3, 1.5, ((0, 2),), jnp.float32),
        "decay_log": jnp.clip(2.77 * jax.random.uniform(streams_of[12], (N_SECTION, H), jnp.float32) ** levels(streams_of[12], (N_SECTION, H), ((0, 2), (1, 4)), -0.2, 0.2), 0.0, 2.77),
        "step_bias": jnp.clip(-5.0 + 4.0 * jax.random.uniform(streams_of[13], (N_SECTION, H), jnp.float32) ** levels(streams_of[13], (N_SECTION, H), ((0, 2), (1, 4)), -0.2, 0.2), -5.0, -1.0),
        "skip_gain": jnp.clip(0.5 + 1.0 * jax.random.uniform(streams_of[14], (N_SECTION, H), jnp.float32) ** levels(streams_of[14], (N_SECTION, H), ((0, 2), (1, 4)), -0.2, 0.2), 0.5, 1.5),
        "mixer_gain": jnp.clip(1.0 + 0.18 * jax.random.normal(streams_of[15], (N_SECTION, DI), jnp.float32), 0.099609375, 1.8984375).astype(jnp.bfloat16),
        "output_weight": noise(streams_of[16], (N_SECTION, DI, D), DI ** -0.5, 0.125, ((0, 2), (1, 4), (2, 16))),
    }


EPSILON = 1e-05
PRECISE = lax.Precision.HIGHEST

@jax.custom_vjp
def low(v):
    return lax.optimization_barrier(v.astype(jnp.bfloat16)).astype(jnp.float32)

@jax.custom_vjp
def low_back(v):
    return v

def low_keep(v):
    return (low(v), None)

def low_pass(kept, grad):
    return (grad,)

def back_keep(v):
    return (v, None)

def back_low(kept, grad):
    return (low(grad),)
low.defvjp(low_keep, low_pass)
low_back.defvjp(back_keep, back_low)

def conv_reset(values, kernel, shift_bias, segment_ids):
    length = values.shape[0]
    kernel_taps = kernel.shape[0]
    total = shift_bias[None, :] + kernel[kernel_taps - 1][None, :] * values
    for back_step in range(1, kernel_taps):
        earlier = jnp.pad(values, ((back_step, 0), (0, 0)))[:length]
        earlier_ids = jnp.pad(segment_ids, (back_step, 0), constant_values=-1)[:length]
        same_doc = (earlier_ids == segment_ids).astype(values.dtype)
        total = total + kernel[kernel_taps - 1 - back_step][None, :] * earlier * same_doc[:, None]
    return total

def group_scan(per_head, step_size, log_decay, input_state, output_state, segment_ids):
    length, head_count, head_size = per_head.shape
    state_size = input_state.shape[1]
    blocks = length // CH
    sliced = (per_head.reshape(blocks, CH, head_count, head_size), step_size.reshape(blocks, CH, head_count), log_decay.reshape(blocks, CH, head_count), input_state.reshape(blocks, CH, state_size), output_state.reshape(blocks, CH, state_size), segment_ids.reshape(blocks, CH))
    lower_mask = jnp.arange(CH)[:, None] >= jnp.arange(CH)[None, :]
    lower_ones = lower_mask.astype(per_head.dtype)

    def advance(carried_in, block_data):
        carried, previous_id = carried_in
        block_x, block_step, block_decay, block_in, block_out, block_ids = block_data
        cum_decay = jnp.dot(lower_ones, block_decay, precision=PRECISE)
        same_doc = (block_ids[:, None] == block_ids[None, :]) & lower_mask
        pair_gap = cum_decay.T[:, :, None] - cum_decay.T[:, None, :]
        pair_decay = jnp.where(same_doc[None], jnp.exp(jnp.where(same_doc[None], pair_gap, 0.0)), 0.0)
        match_scores = jnp.dot(block_out, block_in.T, precision=PRECISE)
        mixing = pair_decay * match_scores[None] * block_step.T[:, None, :]
        within_block = jnp.einsum('hts,shp->thp', mixing, block_x, precision=PRECISE)
        resumes = (block_ids == previous_id).astype(per_head.dtype)
        reach_scale = jnp.exp(cum_decay) * resumes[:, None]
        from_state = jnp.einsum('tn,hpn->thp', block_out, carried, precision=PRECISE) * reach_scale[:, :, None]
        final_id = block_ids[CH - 1]
        tail_weight = jnp.exp(cum_decay[CH - 1][None, :] - cum_decay) * (block_ids == final_id).astype(per_head.dtype)[:, None] * block_step
        fresh_state = jnp.einsum('sh,shp,sn->hpn', tail_weight, block_x, block_in, precision=PRECISE)
        persist = jnp.exp(cum_decay[CH - 1]) * (final_id == previous_id).astype(per_head.dtype)
        carried = persist[:, None, None] * carried + fresh_state
        return ((carried, final_id), within_block + from_state)
    initial = (jnp.zeros((head_count, head_size, state_size), per_head.dtype), jnp.int32(-1))
    _, produced = lax.scan(jax.checkpoint(advance), initial, sliced)
    return produced.reshape(length, head_count, head_size)

def mixer(gate_part, value_part, state_part, step_part, segment_ids, conv_kernel, conv_offset, state_kernel, state_offset, decay_log, step_bias, skip_gain):
    values = jax.nn.silu(conv_reset(value_part, conv_kernel, conv_offset, segment_ids))
    states = jax.nn.silu(conv_reset(state_part, state_kernel, state_offset, segment_ids))
    length = values.shape[0]
    head_count = decay_log.shape[0]
    state_size = states.shape[1] // 2
    per_head = values.reshape(length, head_count, -1)
    step_size = jax.nn.softplus(step_part + step_bias[None, :])
    log_decay = -step_size * jnp.exp(decay_log)[None, :]
    scanned = group_scan(per_head, step_size, log_decay, states[:, :state_size], states[:, state_size:], segment_ids)
    scanned = scanned + skip_gain[None, :, None] * per_head
    return scanned.reshape(length, -1) * jax.nn.silu(gate_part)

def layer(layer_input, segment_ids, weights):
    norm_gain, gate_weight, value_weight, step_weight, state_weight, conv_kernel, conv_offset, state_kernel, state_offset, decay_log, step_bias, skip_gain, mixer_gain, output_weight = weights
    residual = layer_input
    scale_in = lax.rsqrt(lax.optimization_barrier(jnp.mean(residual * residual, axis=-1, keepdims=True)) + EPSILON)
    normed = low(residual * scale_in * norm_gain[None, :])
    gate_part = low_back(jnp.dot(normed, gate_weight, precision=PRECISE))
    value_part = low_back(jnp.dot(normed, value_weight, precision=PRECISE))
    state_part = low_back(jnp.dot(normed, state_weight, precision=PRECISE))
    step_part = low_back(jnp.dot(normed, step_weight, precision=PRECISE))
    gated = mixer(gate_part, value_part, state_part, step_part, segment_ids, conv_kernel, conv_offset, state_kernel, state_offset, decay_log, step_bias, skip_gain)
    scale_mid = lax.rsqrt(lax.optimization_barrier(jnp.mean(gated * gated, axis=-1, keepdims=True)) + EPSILON)
    mixed = low(gated * scale_mid * mixer_gain[None, :])
    branch = low_back(jnp.dot(mixed, output_weight, precision=PRECISE))
    return residual + branch

def reference(tokens, segments, cotangent, norm_gain, gate_weight, value_weight, step_weight, state_weight, conv_kernel, conv_offset, state_kernel, state_offset, decay_log, step_bias, skip_gain, mixer_gain, output_weight):
    params = tuple((weight.astype(jnp.float32) for weight in (norm_gain, gate_weight, value_weight, step_weight, state_weight, conv_kernel, conv_offset, state_kernel, state_offset, decay_log, step_bias, skip_gain, mixer_gain, output_weight)))
    row_total = MICRO * (TOKENS // ROW)
    row_ids = segments.reshape(row_total, ROW)

    def run_section(section_params, section_input):
        flat_rows = section_input.reshape(row_total, ROW, D)

        def one_row(row_pair):
            return layer(row_pair[0], row_pair[1], section_params)
        produced = lax.map(jax.checkpoint(one_row), (flat_rows, row_ids))
        return produced.reshape(MICRO, TOKENS, D)

    def whole_model(section_params, model_input, probe_shift):
        first_params = tuple((weight[0] for weight in section_params))
        second_params = tuple((weight[1] for weight in section_params))
        first_raw = run_section(first_params, model_input)
        second_raw = run_section(second_params, low_back(low(first_raw)) + probe_shift)
        return (second_raw, first_raw)
    inputs = tokens.astype(jnp.float32)
    probe_shift = jnp.zeros_like(inputs)
    (second_out, first_out), pullback = jax.vjp(whole_model, params, inputs, probe_shift)
    param_grads, input_grad, probe_grad = pullback((cotangent.astype(jnp.float32), jnp.zeros_like(first_out)))
    section_outputs = jnp.stack([first_out, second_out])
    input_grads = jnp.stack([input_grad, probe_grad])
    return (section_outputs, input_grads, param_grads[0], param_grads[1], param_grads[2], param_grads[3], param_grads[4], param_grads[5], param_grads[6], param_grads[7], param_grads[8], param_grads[9], param_grads[10], param_grads[11], param_grads[12], param_grads[13])
```

```python
import functools
import types

import jax
import jax.numpy as jnp
from jax import lax
from jax.experimental import pallas as pl
from jax.experimental.pallas import tpu as pltpu
from jax.sharding import PartitionSpec as P

EPSILON = 1e-05
F32 = jnp.float32
BF16 = jnp.bfloat16
MESH = pl.DeviceIdType.MESH
CHUNK = 128
PIECE = 64
PIECES = (0, 1)
CUT = 200.0
SENDS = 64
COPIES = 388
VMEM_LIMIT = 63 * 2**20


def mm(a, b):
    return jnp.dot(a, b, preferred_element_type=F32)


def mm_nt(a, b):
    return lax.dot_general(a, b, (((1,), (1,)), ((), ())), preferred_element_type=F32)


def mm_tn(a, b):
    return lax.dot_general(a, b, (((0,), (0,)), ((), ())), preferred_element_type=F32)


def pieces(a, count):
    out = []
    for _ in range(count):
        part = a.astype(BF16)
        out.append(part)
        a = a - part.astype(F32)
    return out


def exact(product, a, b, count):
    total = None
    for part in pieces(a, count):
        term = product(part, b)
        total = term if total is None else total + term
    return total


def exact_left(product, ones, b, count):
    total = None
    for part in pieces(b, count):
        term = product(ones, part)
        total = term if total is None else total + term
    return total


def iota(dims, dim):
    return lax.broadcasted_iota(jnp.int32, dims, dim)


def spread_matrix(lanes):
    return (iota((CHUNK, lanes), 1) // 64 == iota((CHUNK, lanes), 0)).astype(BF16)


def sigmoid(a):
    return 1.0 / (1.0 + jnp.exp(-a))


def softplus(a):
    return jnp.maximum(a, 0.0) + jnp.log1p(jnp.exp(-jnp.abs(a)))


def row_chunk(c, count=CHUNK):
    return pl.ds(pl.multiple_of(c * CHUNK, CHUNK), count)


def block(index, count):
    return pl.ds(pl.multiple_of(index * count, count), count)


def by_rows(total, step, body):
    def one(i, carry):
        body(pl.ds(pl.multiple_of(i * step, step), step))
        return carry

    lax.fori_loop(0, total // step, one, 0)


def conv(padded, taps, offset, masks, lanes):
    wide = lanes // CHUNK
    total = offset + taps[3] * padded[8:]
    for j in (1, 2, 3):
        m = masks[j - 1]
        m = m if wide == 1 else jnp.concatenate([m] * wide, axis=1)
        total = total + taps[3 - j] * (padded[8 - j : 8 - j + CHUNK] * m)
    return total


def input_grad(dn, u, e, gain):
    r = u.astype(F32)
    scale = lax.rsqrt(jnp.mean(r * r, axis=-1, keepdims=True) + EPSILON)
    weighted = dn * gain
    pull = scale * scale * scale * jnp.mean(r * weighted, axis=-1, keepdims=True)
    return e.astype(F32) + scale * weighted - r * pull


class Links:
    def __init__(self, side, send_ref, recv_ref):
        self.side, self.send_ref, self.recv_ref, self.used, self.open = side, send_ref, recv_ref, 0, []
        self.slots, self.held = list(range(send_ref.shape[0])), set()
        self.section = lax.axis_index("section")
        self.dp = lax.axis_index("dp")
        self.tp = lax.axis_index("tp")
        self.y, self.x = self.dp // side, self.dp % side
        self.far, self.core = self.tp // 2, self.tp % 2

    def along_x(self, k):
        return {"dp": self.y * self.side + (self.x + k) % self.side}

    def along_y(self, k):
        return {"dp": (self.y + k) % self.side * self.side + self.x}

    def other_section(self):
        return {"section": 1 - self.section}

    def along_tp(self, k):
        return {"tp": (self.tp + k) % 4}

    def far_along_tp(self, k):
        return {"section": 1 - self.section, "tp": (self.tp + k) % 4}

    def sibling(self):
        return {"tp": 2 * self.far + 1 - self.core}

    def across(self):
        return {"tp": 2 * (1 - self.far) + self.core}

    def meet(self, partners):
        barrier = pltpu.get_barrier_semaphore()
        for partner in partners:
            pl.semaphore_signal(barrier, inc=1, device_id=partner, device_id_type=MESH)
        pl.semaphore_wait(barrier, len(partners))

    def dp_partners(self):
        return [self.along_x(k) for k in range(1, self.side)] + [self.along_y(k) for k in range(1, self.side)]

    def tp_partners(self):
        return [self.along_tp(k) for k in (1, 2, 3)] + [self.far_along_tp(k) for k in (0, 1, 2, 3)]

    def plan(self, src, dst, to, when=None):
        if not self.slots:
            oldest = next(entry for entry in self.open if id(entry[0]) not in self.held)
            self.sent([oldest[0]])
        slot = self.slots.pop(0)
        copy = pltpu.make_async_remote_copy(
            src_ref=src, dst_ref=dst, send_sem=self.send_ref.at[slot], recv_sem=self.recv_ref.at[self.used],
            device_id=to, device_id_type=MESH,
        )
        self.used += 1
        self.open.append((copy, when, slot))
        return copy

    def send(self, src, dst, to):
        copy = self.plan(src, dst, to)
        copy.start()
        return copy

    def hold(self, copies):
        self.held.update(id(copy) for copy in copies)

    def started(self, copies):
        self.held.difference_update(id(copy) for copy in copies)

    def begin(self, copies):
        for copy in copies:
            self.held.discard(id(copy))
            copy.start()

    def sent(self, copies):
        for copy in copies:
            for i, (other, when, slot) in enumerate(self.open):
                if other is copy:
                    self.leave(copy, when)
                    self.slots.append(slot)
                    del self.open[i]
                    break

    def leave(self, copy, when):
        if when is None:
            copy.wait_send()
        else:
            pl.when(when)(copy.wait_send)

    def finish(self):
        for copy, when, slot in self.open:
            self.leave(copy, when)


def arrived(copies):
    for copy in copies:
        copy.wait_recv()


class Compute:
    def __init__(self, s):
        self.s = s
        self.inner = s.y.shape[2]
        self.pairs = self.inner // CHUNK
        self.width = s.rows.shape[2]

    def weight(self, ref, *at):
        value = ref[at]
        return value.reshape(-1, value.shape[-1])

    def normalise(self, layer, j):
        s = self.s

        def one(rows):
            r = s.rows[layer, rows, :].astype(F32)
            scale = lax.rsqrt(jnp.mean(r * r, axis=-1, keepdims=True) + EPSILON)
            s.rows[layer, rows, :] = (r * scale * s.p[layer, 6:7, :]).astype(BF16)

        for k in (0, 1):
            by_rows_from(256 * j + CHUNK * k, CHUNK, 64, one)

    def project(self, layer, j):
        s = self.s
        rows = pl.ds(256 * j, 256)
        normed = s.rows[layer, rows, :]
        down = pl.ds(8 + 256 * j, 256)
        for h in (0, 1):
            s.v[layer, down, pl.ds(256 * h, 256)] = mm(normed, self.weight(s.wv, layer, h))
            s.bc[layer, down, pl.ds(128 * h, 128)] = mm(normed, self.weight(s.ws, layer, h))
        s.q[layer, rows, :] = mm_nt(normed, s.wq[layer])

    def gate_input(self, layer, j):
        s = self.s
        rows = pl.ds(256 * j, 256)
        s.z[layer, rows, :] = mm(s.rows[layer, rows, :], self.weight(s.wz, layer))

    def upstream(self, layer, j):
        s = self.s
        rows = pl.ds(256 * j, 256)
        s.dy[rows, :] = mm(s.e[layer, rows, :], self.weight(s.wo, layer))

    def start_forward(self, layer):
        s = self.s
        s.state[...] = jnp.zeros_like(s.state)
        s.v[layer, 0:8, :] = jnp.zeros((8, self.inner), F32)
        s.bc[layer, 0:8, :] = jnp.zeros((8, 256), F32)

    def steps(self, layer, rows, boundary, lower):
        s = self.s
        pre = s.q[layer, rows, :] + s.p[layer, 7:8, 128:256]
        dt = softplus(pre)
        rate = jnp.exp(s.p[layer, 7:8, 0:128])
        ld = -dt * rate
        cum = exact_left(mm, lower, ld - CUT * boundary, 3)
        return pre, dt, rate, ld, cum

    def taps(self, layer, lanes):
        p = self.s.p
        return [p[layer, k : k + 1, lanes] for k in range(4)], p[layer, 4:5, lanes]

    def spreads(self, dt, cum, spread):
        last = cum[CHUNK - 1 : CHUNK]
        wide = exact(mm, jnp.concatenate([dt, jnp.exp(cum), jnp.exp(last - cum)], axis=0), spread, 2)
        return wide[0:CHUNK], wide[CHUNK : 2 * CHUNK], wide[2 * CHUNK :]

    def scan(self, layer, j):
        s = self.s

        def chunk(i, carry):
            c = 2 * j + i
            rows = row_chunk(c)
            low = iota((CHUNK, CHUNK), 0) >= iota((CHUNK, CHUNK), 1)
            lower = low.astype(BF16)
            spread = spread_matrix(self.inner)
            first_half = iota((CHUNK, CHUNK), 1) < 64
            seg = s.seg[row_chunk(c, 136), :]
            masks = [(seg[8 - k : 8 - k + CHUNK] == seg[8:]).astype(F32) for k in (1, 2, 3)]
            pre, dt, rate, ld, cum = self.steps(layer, rows, 1.0 - masks[0], lower)
            dt_w, reach_w, tail_w = self.spreads(dt, cum, spread)
            cum_t = cum.T
            bc = conv(s.bc[layer, row_chunk(c, 136), :], *self.taps(layer, slice(512, 768)), masks, 256)
            bc = (bc * sigmoid(bc)).astype(BF16)
            b_low, c_low = bc[:, :CHUNK], bc[:, CHUNK:]
            match = mm_nt(c_low, b_low)
            for p in range(self.pairs):
                lanes = slice(p * CHUNK, (p + 1) * CHUNK)
                pre_x = conv(s.v[layer, row_chunk(c, 136), lanes], *self.taps(layer, lanes), masks, CHUNK)
                x = pre_x * sigmoid(pre_x)
                xd = x * dt_w[:, lanes]
                xd_low = xd.astype(BF16)
                mixing = []
                for h in (2 * p, 2 * p + 1):
                    gap = jnp.where(low, cum[:, h : h + 1] - cum_t[h : h + 1, :], -1e30)
                    mixing.append((match * jnp.exp(gap)).astype(BF16))
                zero = jnp.zeros_like(xd_low)
                halves = jnp.concatenate([jnp.where(first_half, xd_low, zero), jnp.where(first_half, zero, xd_low)], axis=0)
                state = s.state[:, lanes]
                state_low = state.astype(BF16)
                s.kept[layer, c, :, lanes] = state_low
                y = mm(jnp.concatenate(mixing, axis=1), halves) + reach_w[:, lanes] * mm(c_low, state_low)
                s.state[:, lanes] = state * reach_w[CHUNK - 1 : CHUNK, lanes] + mm_tn(b_low, (xd * tail_w[:, lanes]).astype(BF16))
                s.y[layer, rows, lanes] = y + s.p[layer, 7:8, 512 + p * CHUNK : 512 + (p + 1) * CHUNK] * x
            return carry

        lax.fori_loop(0, 2, chunk, 0)

    def gate(self, layer, j, part):
        s = self.s

        def chunk(i, carry):
            rows = row_chunk(2 * j + i)
            squares = cross = None
            for p in range(self.pairs):
                lanes = slice(p * CHUNK, (p + 1) * CHUNK)
                z = s.z[layer, rows, lanes]
                g = s.y[layer, rows, lanes] * (z * sigmoid(z))
                gained = g * s.p[layer, 5:6, lanes]
                s.mixed[rows, lanes] = gained.astype(BF16)
                squares = g * g if squares is None else squares + g * g
                if layer == 1:
                    term = gained * s.dy[rows, lanes]
                    cross = term if cross is None else cross + term
            ones = jnp.ones((8, CHUNK), BF16)
            sums = exact_left(mm_nt, ones, squares, 3)
            if layer == 1:
                sums = jnp.where(iota((8, CHUNK), 0) < 4, sums, exact_left(mm_nt, ones, cross, 3))
            s.stat[layer, :, rows] = sums
            return carry

        lax.fori_loop(0, 2, chunk, 0)
        rows = pl.ds(256 * j, 256)
        mixed = s.mixed[rows, :]
        for n in range(s.wo.shape[1]):
            part[rows, pl.ds(n * 256, 256)] = mm_nt(mixed, self.weight(s.wo, layer, n)).astype(BF16)

    def middle(self, layer, j):
        s = self.s
        lanes = pl.ds(256 * j, 256)
        total = s.stat[layer, :, lanes]
        for k in range(3):
            total = total + s.stat_in[layer, k, :, lanes]
        scale = lax.rsqrt(total / (4.0 * self.inner) + EPSILON)
        s.mid[layer, :, lanes] = jnp.where(iota((8, 256), 0) < 4, scale, total)

    def add_row(self, layer, k, lanes, value):
        self.s.dp[layer, k : k + 1, lanes] += jnp.sum(value, axis=0, keepdims=True)

    def gate_back(self, layer, j):
        s = self.s

        def chunk(i, carry):
            rows = row_chunk(2 * j + i)
            columns = s.mid[layer, :, rows].T
            scale = columns[:, 0:1]
            cross = columns[:, 4:5] if layer == 1 else s.cross[:, rows].T[:, 0:1]
            pull = scale * scale * scale * cross / (4.0 * self.inner)
            for p in range(self.pairs):
                lanes = slice(p * CHUNK, (p + 1) * CHUNK)
                z, y, dmix = s.z[layer, rows, lanes], s.y[layer, rows, lanes], s.dy[rows, lanes]
                gain = s.p[layer, 5:6, lanes]
                sig = sigmoid(z)
                silu = z * sig
                g = y * silu
                scaled = g * scale
                self.add_row(layer, 5, lanes, dmix * scaled)
                s.mixed[rows, lanes] = (scaled * gain).astype(BF16)
                dg = scale * (dmix * gain) - g * pull
                s.dproj[rows, lanes] = (dg * y * (sig * (1.0 + z * (1.0 - sig)))).astype(BF16)
                s.dy[rows, lanes] = dg * silu
            return carry

        lax.fori_loop(0, 2, chunk, 0)

    def start_back(self):
        s = self.s
        s.later[...] = jnp.zeros_like(s.later)
        s.state[...] = jnp.zeros_like(s.state)

    def conv_back(self, layer, c, now, later_lanes, in_ref, lanes, param_lanes, masks_ext, masks):
        s = self.s
        ext = jnp.concatenate([now, s.later[:, later_lanes]], axis=0)
        s.later[:, later_lanes] = now[0:8]
        back = in_ref[layer, row_chunk(c, 136), lanes]
        taps, _ = self.taps(layer, param_lanes)
        total = taps[3] * now
        self.add_row(layer, 4, param_lanes, now)
        self.add_row(layer, 3, param_lanes, now * back[8:])
        for k in (1, 2, 3):
            total = total + taps[3 - k] * (ext * masks_ext[k - 1])[k : k + CHUNK]
            self.add_row(layer, 3 - k, param_lanes, now * (back[8 - k : 8 - k + CHUNK] * masks[k - 1]))
        return total

    def scan_back(self, layer, j):
        s = self.s
        inner = self.inner

        def chunk(i, carry):
            c = 2 * j + 1 - i
            rows = row_chunk(c)
            low = iota((CHUNK, CHUNK), 0) >= iota((CHUNK, CHUNK), 1)
            lower = low.astype(BF16)
            spread = spread_matrix(inner)
            first_half = iota((CHUNK, CHUNK), 1) < 64
            seg = s.seg[row_chunk(c, 144), :]
            masks_ext = [(seg[8 - k : 144 - k] == seg[8:]).astype(F32) for k in (1, 2, 3)]
            masks = [m[0:CHUNK] for m in masks_ext]
            pre_q, dt, rate, ld, cum = self.steps(layer, rows, 1.0 - masks[0], lower)
            dt_w, reach_w, tail_w = self.spreads(dt, cum, spread)
            cum_t = cum.T
            pre_bc = conv(s.bc[layer, row_chunk(c, 136), :], *self.taps(layer, slice(512, 768)), masks, 256)
            sig_bc = sigmoid(pre_bc)
            bc = (pre_bc * sig_bc).astype(BF16)
            b_low, c_low = bc[:, :CHUNK], bc[:, CHUNK:]
            match = mm_nt(c_low, b_low)
            d_match = jnp.zeros((CHUNK, CHUNK), F32)
            d_b = jnp.zeros((CHUNK, CHUNK), F32)
            d_c = jnp.zeros((CHUNK, CHUNK), F32)
            d_cum = jnp.zeros((CHUNK, CHUNK), F32)
            d_dt = jnp.zeros((CHUNK, CHUNK), F32)
            d_end = jnp.zeros((8, CHUNK), F32)
            for p in range(self.pairs):
                lanes = slice(p * CHUNK, (p + 1) * CHUNK)
                skip_lanes = slice(512 + p * CHUNK, 512 + (p + 1) * CHUNK)
                skip = s.p[layer, 7:8, skip_lanes]
                y, dy = s.y[layer, rows, lanes], s.dy[rows, lanes]
                dy_low = dy.astype(BF16)
                pre_x = conv(s.v[layer, row_chunk(c, 136), lanes], *self.taps(layer, lanes), masks, CHUNK)
                sig_x = sigmoid(pre_x)
                x = pre_x * sig_x
                xd = x * dt_w[:, lanes]
                xd_low = xd.astype(BF16)
                zero = jnp.zeros_like(dy_low)
                dy_halves = [jnp.where(first_half, dy_low, zero), jnp.where(first_half, zero, dy_low)]
                mixing = []
                for k in (0, 1):
                    h = 2 * p + k
                    gap = jnp.where(low, cum[:, h : h + 1] - cum_t[h : h + 1, :], -1e30)
                    decay = jnp.exp(gap)
                    mixing.append((match * decay).astype(BF16))
                    d_match = d_match + mm_nt(dy_halves[k], xd_low) * decay
                d_state = s.state[:, lanes]
                d_state_low = d_state.astype(BF16)
                state_low = s.kept[layer, c, :, lanes]
                dxd_tail = tail_w[:, lanes] * mm(b_low, d_state_low)
                dxd = mm_tn(jnp.concatenate(mixing, axis=0), jnp.concatenate(dy_halves, axis=0)) + dxd_tail
                xd_f = xd_low.astype(F32)
                spread_p = spread[:, lanes]
                d_cum = d_cum + exact(mm_nt, dy_low.astype(F32) * (y - skip * x) - xd_f * dxd, spread_p, 3)
                d_dt = d_dt + exact(mm_nt, x * dxd, spread_p, 2)
                end = jnp.sum(xd_f * dxd_tail, axis=0, keepdims=True) + reach_w[CHUNK - 1 : CHUNK, lanes] * jnp.sum(
                    state_low.astype(F32) * d_state, axis=0, keepdims=True
                )
                d_end = d_end + exact(mm_nt, jnp.broadcast_to(end, (8, CHUNK)), spread_p, 3)
                dx = dt_w[:, lanes] * dxd + skip * dy
                self.add_row(layer, 7, skip_lanes, dy * x)
                dpre_x = dx * (sig_x * (1.0 + pre_x * (1.0 - sig_x)))
                dy_reach = (dy * reach_w[:, lanes]).astype(BF16)
                d_c = d_c + mm_nt(dy_reach, state_low)
                d_b = d_b + mm_nt((xd * tail_w[:, lanes]).astype(BF16), d_state_low)
                s.state[:, lanes] = d_state * reach_w[CHUNK - 1 : CHUNK, lanes] + mm_tn(c_low, dy_reach)
                dv = self.conv_back(layer, c, dpre_x, lanes, s.v, lanes, lanes, masks_ext, masks)
                s.dproj[rows, inner + p * CHUNK : inner + (p + 1) * CHUNK] = dv.astype(BF16)
            d_match_low = d_match.astype(BF16)
            d_c = d_c + mm(d_match_low, b_low)
            d_b = d_b + mm_tn(d_match_low, c_low)
            d_ld = exact_left(mm_tn, lower, d_cum, 3) + d_end[0:1]
            self.add_row(layer, 7, slice(0, 128), d_ld * ld)
            d_q = (d_dt - d_ld * rate) * sigmoid(pre_q)
            self.add_row(layer, 7, slice(128, 256), d_q)
            s.dproj[rows, 2 * inner + 256 :] = d_q.astype(BF16)
            d_bc = jnp.concatenate([d_b, d_c], axis=1)
            d_bc = d_bc * (sig_bc * (1.0 + pre_bc * (1.0 - sig_bc)))
            for k in (0, 1):
                lanes = slice(k * CHUNK, (k + 1) * CHUNK)
                param_lanes = slice(512 + k * CHUNK, 512 + (k + 1) * CHUNK)
                d_in = self.conv_back(layer, c, d_bc[:, lanes], param_lanes, s.bc, lanes, param_lanes, masks_ext, masks)
                s.dproj[rows, 2 * inner + k * CHUNK : 2 * inner + (k + 1) * CHUNK] = d_in.astype(BF16)
            return carry

        lax.fori_loop(0, 2, chunk, 0)

    def normed_grad(self, layer, j, part):
        s = self.s
        inner = self.inner
        rows = pl.ds(256 * j, 256)
        grad = lambda first, count: s.dproj[rows, first : first + count]
        for n in range(s.wz.shape[1]):
            lanes = slice(n * 256, (n + 1) * 256)
            total = mm_nt(grad(0, inner), self.weight(s.wz, layer, n)) + mm(grad(2 * inner + 256, 128), s.wq[layer, :, lanes])
            for h in (0, 1):
                total = total + mm_nt(grad(inner + 256 * h, 256), self.weight(s.wv, layer, h, n))
                total = total + mm_nt(grad(2 * inner + 128 * h, 128), self.weight(s.ws, layer, h, n))
            part[rows, lanes] = total.astype(BF16)
            self.add_row(layer, 6, lanes, total * s.rows[layer, rows, lanes].astype(F32) / s.p[layer, 6:7, lanes])

    def weight_grad(self, layer, out, left, right, half=()):
        for n in range(self.s.dz.shape[1]):
            value = mm_tn(left[layer, :, pl.ds(n * 256, 256)], right)
            at = (layer,) + half + (n,)
            out[at] = value.astype(BF16).reshape(out.shape[len(at) :])

    def step_grad(self, layer):
        s = self.s
        s.dt[layer] = mm_tn(s.dproj[:, 2 * self.inner + 256 :], s.rows[layer])[0:8]


def by_rows_from(first, total, step, body):
    def one(i, carry):
        body(pl.ds(pl.multiple_of(first + i * step, step), step))
        return carry

    lax.fori_loop(0, total // step, one, 0)


class RowStage:
    def __init__(self, links, s, g, j, part, gathered=None):
        self.links, self.s, self.g, self.j, self.part = links, s, g, j, part
        self.owner = links.far == j
        self.helper = links.far != j
        mine, theirs = 2 * j + links.core, 2 * j + 1 - links.core
        self.rows = [block(2 * mine + h, PIECE) for h in PIECES]
        piece = [pl.ds(h * PIECE, PIECE) for h in PIECES]
        self.piece = piece
        self.pair = [
            links.plan(part.at[block(2 * theirs + h, PIECE)], s.sib.at[g, j, piece[h]], links.sibling()) for h in PIECES
        ]
        self.over = [
            links.plan(s.chip.at[g, j, piece[h]], s.chip.at[g, j, piece[h]], links.across(), self.helper) for h in PIECES
        ]
        links.hold(self.pair + self.over)
        if gathered is not None:
            views = [gathered.at[r] for r in self.rows]
            self.views = views
            self.give = [links.plan(v, v, links.across(), self.owner) for v in views]
            self.share = [links.plan(v, v, links.sibling(), self.owner) for v in views]
            self.hand = [links.plan(v, v, links.sibling(), self.helper) for v in views]
            links.hold(self.give + self.share + self.hand)

    def start(self):
        self.links.begin(self.pair)

    def cross(self):
        for h in PIECES:
            self.pair[h].wait_recv()

        @pl.when(self.helper)
        def _():
            for h in PIECES:
                total = self.part[self.rows[h], :].astype(F32) + self.s.sib[self.g, self.j, self.piece[h], :].astype(F32)
                self.s.chip[self.g, self.j, self.piece[h], :] = total.astype(BF16)
                self.links.begin([self.over[h]])

    def total(self, make, after=None):
        @pl.when(self.owner)
        def _():
            for h in PIECES:
                self.over[h].wait_recv()
                total = self.part[self.rows[h], :].astype(F32) + self.s.sib[self.g, self.j, self.piece[h], :].astype(F32)
                result = make(h, total + self.s.chip[self.g, self.j, self.piece[h], :].astype(F32))
                if result is not None:
                    self.views[h][...] = result
                    self.links.begin([self.give[h], self.share[h]])
            if after is not None:
                after()

    def collect(self):
        @pl.when(self.helper)
        def _():
            for h in PIECES:
                self.give[h].wait_recv()
                self.links.begin([self.hand[h]])
            for h in PIECES:
                self.hand[h].wait_recv()

        @pl.when(self.owner)
        def _():
            for h in PIECES:
                self.share[h].wait_recv()

    def release(self):
        self.links.sent(self.give + self.share + self.hand)


class RowGather:
    def __init__(self, links, own, gathered):
        self.links = links
        self.over, self.pair, self.pass_on = [], [], []
        for h in PIECES:
            rows = block(2 * links.tp + h, PIECE)
            other = gathered.at[block(2 * (2 * (1 - links.far) + links.core) + h, PIECE)]
            self.over.append(links.plan(own.at[pl.ds(h * PIECE, PIECE)], gathered.at[rows], links.across()))
            self.pair.append(links.plan(own.at[pl.ds(h * PIECE, PIECE)], gathered.at[rows], links.sibling()))
            self.pass_on.append(links.plan(other, other, links.sibling()))
        links.hold(self.over + self.pair + self.pass_on)

    def start(self):
        self.links.begin(self.over + self.pair)

    def forward(self):
        for h in PIECES:
            self.over[h].wait_recv()
            self.links.begin([self.pass_on[h]])

    def collect(self):
        arrived(self.pair + self.pass_on)

    def release(self):
        self.links.sent(self.over + self.pair + self.pass_on)


class RingGather:
    def __init__(self, links, view, me, to):
        self.links, self.view, self.me, self.to = links, view, me, to

    def start(self):
        self.up, self.down = {}, {}
        for h in (0, 1):
            for moves, half, k in ((self.up, h, 1), (self.down, 1 - h, -1)):
                at = self.view(self.me, half)
                moves[half] = self.links.send(at, at, self.to(k))

    def pass_on(self):
        side = self.links.side
        self.up[0].wait_recv()
        at = self.view((self.me + side - 1) % side, 0)
        self.last = [self.links.send(at, at, self.to(1))]
        self.down[1].wait_recv()
        at = self.view((self.me + 1) % side, 1)
        self.last.append(self.links.send(at, at, self.to(-1)))

    def end(self):
        arrived([self.up[1], self.down[0]] + self.last)


class RingSum:
    def __init__(self, links, view, far, near, me, to):
        self.links, self.view, self.far, self.near, self.me, self.to = links, view, far, near, me, to

    def start(self):
        links, side, me = self.links, self.links.side, self.me
        across = (me + 2) % side
        self.through = [
            links.send(self.view(across, 0), self.far.at[0], self.to(1)),
            links.send(self.view(across, 1), self.far.at[1], self.to(-1)),
        ]
        self.direct = [
            links.send(self.view((me + 1) % side, 1), self.near.at[0, 1], self.to(1)),
            links.send(self.view((me + side - 1) % side, 0), self.near.at[1, 0], self.to(-1)),
        ]

    def pass_on(self):
        links, side, me = self.links, self.links.side, self.me
        for h, k in ((0, 1), (1, -1)):
            self.through[h].wait_recv()
            mine = self.view((me + side + k) % side, h)
            add_blocks(self.far.at[h], [mine, self.far.at[h]])
            self.direct.append(links.send(self.far.at[h], self.near.at[h, h], self.to(k)))

    def end(self, out):
        arrived(self.direct)
        for h in (0, 1):
            each_block([self.view(self.me, h), self.near.at[0, h], self.near.at[1, h]], functools.partial(out, h))


def each_block(refs, out):
    dims = refs[0].shape
    if len(dims) == 3:
        for i in range(dims[0]):
            each_block([r.at[i] for r in refs], lambda at, total, i=i: out((i,) + at, total))
        return

    def one(rows):
        total = refs[0][rows, :].astype(F32)
        for ref in refs[1:]:
            total = total + ref[rows, :].astype(F32)
        out((rows,), total)

    by_rows(dims[0], 32, one)


def add_blocks(out, refs):
    def put(at, total):
        out[at + (slice(None),)] = total.astype(BF16)

    each_block(refs, put)


def spread_over_dp(links, ref, along):
    y, x = links.y, links.x
    own = ref.at[y, x]
    if along == "x":
        one = [links.send(own, own, links.along_x(k)) for k in (1, 2, 3)]
        two = RingGather(links, lambda i, h: ref.at[i, pl.ds(2 * h, 2)], y, links.along_y)
    else:
        one = [links.send(own, own, links.along_y(k)) for k in (1, 2, 3)]
        two = RingGather(links, lambda i, h: ref.at[pl.ds(2 * h, 2), i], x, links.along_x)
    yield
    arrived(one)
    two.start()
    yield
    two.pass_on()
    yield
    two.end()
    yield


def flow_over_dp(links, ref, along):
    y, x, side = links.y, links.x, links.side
    if along == "x":
        first, second, me, view = links.along_x, links.along_y, x, lambda k, way: ref.at[(y + side + way) % side, (x + side - k) % side]
    else:
        first, second, me, view = links.along_y, links.along_x, y, lambda k, way: ref.at[(y + side - k) % side, (x + side + way) % side]
    up, down, last = {}, {}, []

    def both(k):
        at = view(k, 0)
        up[k], down[k] = links.send(at, at, second(1)), links.send(at, at, second(-1))

    def pass_on(k):
        if k in (0, 3):
            up[k].wait_recv()
            at = view(k, -1)
            last.append(links.send(at, at, second(1)))
        else:
            down[k].wait_recv()
            at = view(k, 1)
            last.append(links.send(at, at, second(-1)))

    own = view(0, 0)
    one = {k: links.send(own, own, first(k)) for k in (1, 3, 2)}
    both(0)
    yield
    for k in (1, 3, 2):
        one[k].wait_recv()
        both(k)
    yield
    pass_on(0)
    yield
    for k in (1, 3, 2):
        pass_on(k)
    yield
    arrived([(down if k in (0, 3) else up)[k] for k in (0, 1, 3, 2)] + last)
    yield


def spread_small(links, ref):
    own = ref.at[links.y, links.x]
    one = [links.send(own, own, links.along_x(k)) for k in (1, 2, 3)]
    yield
    arrived(one)
    own = ref.at[links.y]
    two = [links.send(own, own, links.along_y(k)) for k in (1, 2, 3)]
    yield
    yield
    arrived(two)
    yield


def sum_over_dp(links, grad, far, near, mid, second_in, along, out):
    y, x, side = links.y, links.x, links.side
    if along == "y":
        view, me, place, to = lambda i, h: grad.at[i, pl.ds(2 * h, 2)], y, x, (links.along_y, links.along_x)
    else:
        view, me, place, to = lambda i, h: grad.at[pl.ds(2 * h, 2), i], x, y, (links.along_x, links.along_y)
    one = RingSum(links, view, far, near, me, to[0])

    def put(h, at, total):
        i, rows = at
        mid[2 * h + i, rows, :] = total.astype(BF16)

    one.start()
    yield
    one.pass_on()
    yield
    one.end(put)
    two = [links.send(mid.at[(place + k) % side], second_in.at[k - 1], to[1](k)) for k in (1, 2, 3)]
    yield
    arrived(two)
    each_block([mid.at[place]] + [second_in.at[k] for k in range(3)], lambda at, total: out(at[0], total))
    yield


def step(*tasks):
    for task in tasks:
        next(task)


def when_arrived(copies, condition):
    @pl.when(condition)
    def _():
        arrived(copies)


def start_when(links, copies, condition):
    @pl.when(condition)
    def _():
        links.begin(copies)


def prepare(s, links):
    sec, y, x = links.section, links.y, links.x
    s.wz[sec, y, x] = s.gate_weight[0]
    for h in (0, 1):
        s.wv[sec, h, y, x] = s.value_weight[0, :, 256 * h : 256 * (h + 1)]
    s.wo[sec, y, x] = s.out_weight[...]
    s.ws[sec, links.core, y, x] = s.state_weight[0, :, block(links.core, 128)]
    heads, depth = s.step_weight.shape[1:]
    s.tiny[...] = jnp.zeros_like(s.tiny)
    s.tiny[0:heads, 0:depth] = s.step_weight[0].astype(F32)
    tile = s.tiny[...]
    s.wt[sec, y, x] = jnp.where(x % 2 == 0, tile, pltpu.roll(tile, depth, 1))
    s.wq[...] = jnp.zeros_like(s.wq)
    inner = s.y.shape[2]
    s.p[sec] = jnp.zeros(s.p.shape[1:], F32)
    s.p[sec, 0:4, 0:inner] = s.conv_kernel[0]
    s.p[sec, 0:4, inner : inner + 256] = s.state_kernel[0]
    s.p[sec, 4:5, 0:inner] = s.conv_offset[...]
    s.p[sec, 4:5, inner : inner + 256] = s.state_offset[...]
    s.p[sec, 5:6, 0:inner] = s.mixer_gain[...].astype(F32)
    s.p[sec, 6:7, :] = s.norm_gain[...].astype(F32)
    s.p[sec, 7:8, 0:heads] = s.decay_log[...]
    s.p[sec, 7:8, 128 : 128 + heads] = s.step_bias[...]
    s.tiny[...] = jnp.zeros_like(s.tiny)
    s.tiny[0:1, 0:heads] = s.skip_gain[...]
    s.p[sec, 7:8, 512:] = exact(mm, s.tiny[...], spread_matrix(inner), 3)[0:1]
    s.dp[...] = jnp.zeros_like(s.dp)
    s.seg[0:8, :] = jnp.full((8, CHUNK), -1.0, F32)
    total = s.seg.shape[0] - 16
    s.seg[total + 8 :, :] = jnp.full((8, CHUNK), -1.0, F32)
    line = jnp.where(sec == 0, s.segments[0:1, :], s.segments[1:2, :]).astype(F32)
    for c in range(total // CHUNK):
        s.seg[8 + c * CHUNK : 8 + (c + 1) * CHUNK, :] = jnp.broadcast_to(line[:, c * CHUNK : (c + 1) * CHUNK], (CHUNK, CHUNK)).T


def relay_body(side, names, *refs):
    s = types.SimpleNamespace(**dict(zip(names, refs)))
    links = Links(side, s.send_sem, s.recv_sem)
    work = Compute(s)
    sec, tp = links.section, links.tp
    prepare(s, links)
    links.meet(links.dp_partners() + links.tp_partners() + [links.other_section()])

    core = links.core
    own = block(tp, 2 * PIECE)

    def swap(layer, refs):
        out = [links.plan(ref, ref, links.other_section(), sec == layer) for ref in refs]
        links.hold(out)
        return out

    at = lambda ref, l: ref.at[l, links.y, links.x]
    first_swap = [swap(l, (s.wv.at[l, :, links.y, links.x], s.ws.at[l, core, links.y, links.x], at(s.wt, l), s.p.at[l])) for l in (0, 1)]
    second_swap = [swap(l, (at(s.wz, l), at(s.wo, l))) for l in (0, 1)]
    start_when(links, first_swap[0] + second_swap[0], sec == 0)
    tokens = RowGather(links, s.tokens.at[sec], s.rows.at[0])
    s.rows[0, own, :] = s.tokens[sec]
    s.e[1, own, :] = s.cotangent[sec]
    spread = (flow_over_dp, spread_over_dp)
    scan_weights = [
        [spread[l](links, s.wv.at[l, 0], "x"), spread[l](links, s.wv.at[l, 1], "y"), spread[l](links, s.ws.at[l, core], "y")] for l in (0, 1)
    ]
    step_weights = [spread_small(links, s.wt.at[l]) for l in (0, 1)]
    gate_weights = [[spread[l](links, s.wz.at[l], "x"), spread[l](links, s.wo.at[l], "y")] for l in (0, 1)]

    def end_scan_weights(l):
        step(*scan_weights[l], step_weights[l])
        shared = links.send(s.ws.at[l, core], s.ws.at[l, core], links.sibling())
        for i in range(side):
            for k in range(side // 2):
                tile = s.wt[l, i, 2 * k] + s.wt[l, i, 2 * k + 1]
                n = (i * side // 2 + k) * 128
                s.wq[l, 0:16, n : n + 128] = jnp.concatenate([tile, jnp.zeros_like(tile)], axis=0).astype(BF16)
        shared.wait_recv()

    when_arrived(first_swap[0], sec == 1)
    step(*scan_weights[0], step_weights[0])
    when_arrived(second_swap[0], sec == 1)
    step(*gate_weights[0])
    tokens.start()
    step(*scan_weights[0], step_weights[0])
    step(*scan_weights[0])
    step(*gate_weights[0])
    step(*scan_weights[0])
    step(*gate_weights[0])
    tokens.forward()
    start_when(links, first_swap[1] + second_swap[1], sec == 1)
    cotangent = RowGather(links, s.cotangent.at[sec], s.e.at[1])
    tokens.collect()
    tokens.release()
    for j in (0, 1):
        work.normalise(0, j)
    step(step_weights[0])
    end_scan_weights(0)
    step(*gate_weights[0])
    work.start_forward(0)
    work.project(0, 0)
    work.scan(0, 0)
    when_arrived(first_swap[1] + second_swap[1], sec == 0)
    step(*scan_weights[1], step_weights[1])
    step(*gate_weights[1])
    cotangent.start()
    work.project(0, 1)
    work.scan(0, 1)
    step(*gate_weights[0])

    def stats(layer, j):
        at = pl.ds(256 * j, 256)
        return [links.send(s.stat.at[layer, :, at], s.stat_in.at[layer, k - 1, :, at], links.along_tp(k)) for k in (1, 2, 3)]

    def own_scale(layer):
        return s.mid[layer, :, own].T[:, 0:1]

    def first_out(h, total):
        rows = slice(h * PIECE, (h + 1) * PIECE)
        s.tot[rows, :] = total
        result = s.tokens[sec, rows, :].astype(F32) + total * own_scale(0)[rows]
        s.res[0, rows, :] = result
        return result.astype(BF16)

    def second_out(h, total):
        rows = slice(h * PIECE, (h + 1) * PIECE)
        s.res[1, rows, :] = s.res[0, rows, :].astype(BF16).astype(F32) + total * own_scale(1)[rows]

    stages = {}
    moved = {}
    part = [s.part.at[0], s.part.at[1]]
    for j in (0, 1):
        work.gate_input(0, j)
        work.gate(0, j, part[0])
        moved[0, j] = stats(0, j)
        stages[0, j] = RowStage(links, s, 0, j, part[0], s.rows.at[1])
        stages[0, j].start()
    step(*scan_weights[1], step_weights[1])
    for j in (0, 1):
        stages[0, j].cross()
    step(*gate_weights[1])
    for j in (0, 1):
        arrived(moved[0, j])
        work.middle(0, j)
    cotangent.forward()
    step(*scan_weights[1], step_weights[1])
    for j in (0, 1):
        stages[0, j].total(first_out)
    step(*gate_weights[1])
    work.start_forward(1)
    for j in (0, 1):
        stages[0, j].collect()
        stages[0, j].release()
        work.normalise(1, j)
        if j == 0:
            end_scan_weights(1)
        work.project(1, j)
        work.scan(1, j)
    cotangent.collect()
    step(*gate_weights[1])
    for j in (0, 1):
        work.upstream(1, j)
        work.gate_input(1, j)
        work.gate(1, j, part[1])
        moved[1, j] = stats(1, j)
        stages[1, j] = RowStage(links, s, 1, j, part[1])
        stages[1, j].start()

    across = {}
    inner = work.inner
    arrays = {
        "z": (s.dz.at, "y", s.fz, s.gz), "o": (s.do.at, "x", s.fo, s.go), "v0": (s.dv.at, "y", s.fv, s.gv), "v1": (s.dv.at, "x", s.fv, s.gv),
        "s": (s.ds.at, "x", s.fst, None),
    }

    def sum_of(layer, name):
        grad, along, ref, _ = arrays[name]
        half = {"v0": 0, "v1": 1, "s": core}.get(name)
        grad = grad[layer] if half is None else grad[layer, half]

        def out(rows, total):
            if name == "s":
                ref[layer, rows, :] = total
            elif half is None:
                ref[layer, rows, :] = total.astype(BF16)
            else:
                ref[layer, half, rows, :] = total.astype(BF16)

        get = lambda kind: getattr(s, kind + name).at[layer]
        return sum_over_dp(links, grad, get("a"), get("b"), get("m"), get("c"), along, out)

    def weight_grads(layer, names, tasks):
        for name in names:
            if name == "z":
                work.weight_grad(layer, s.dz, s.rows, s.dproj[:, 0:inner])
            elif name == "o":
                work.weight_grad(layer, s.do, s.e, s.mixed[...])
            elif name == "s":
                for h in (0, 1):
                    work.weight_grad(layer, s.ds, s.rows, s.dproj[:, 2 * inner + 128 * h : 2 * inner + 128 * (h + 1)], (h,))
                across[layer, "core"] = links.send(s.ds.at[layer, 1 - core], s.ds_pair.at[layer], links.sibling())
                work.step_grad(layer)
                continue
            else:
                h = int(name[1])
                first = inner + 256 * h
                work.weight_grad(layer, s.dv, s.rows, s.dproj[:, first : first + 256], (h,))
            tasks[name] = sum_of(layer, name)
            step(tasks[name])

    def start_state_sum(layer, tasks):
        across[layer, "core"].wait_recv()
        for i in range(side):
            add_blocks(s.ds.at[layer, core, i], [s.ds.at[layer, core, i], s.ds_pair.at[layer, i]])
        tasks["s"] = sum_of(layer, "s")
        step(tasks["s"])

    def steps_of(tasks, names):
        step(*[tasks[name] for name in names])

    def end_sums(layer, tasks, names):
        for name in names:
            step(tasks[name])
            if name == "s":
                shard = lambda k: s.fst.at[layer, block((tp + k) % 4, 16)]
                mine = [links.plan(shard(k), s.fst_in.at[layer, k - 1], links.along_tp(k), sec == layer) for k in (1, 2, 3)]
                theirs = [links.plan(shard(k), s.fst_in.at[layer, 3 + k], links.far_along_tp(k), sec != layer) for k in (0, 1, 2, 3)]
                links.hold(mine + theirs)
                start_when(links, mine, sec == layer)
                start_when(links, theirs, sec != layer)
                across[layer, "s"] = mine + theirs
                continue
            ref, far_in = arrays[name][2:]
            view = lambda r: r.at[layer] if name in "zo" else r.at[layer, int(name[1])]
            across[layer, name] = links.plan(view(ref), view(far_in), links.other_section(), sec != layer)
            start_when(links, [across[layer, name]], sec != layer)

    def end_state(layer):
        @pl.when(sec == layer)
        def _():
            arrived(across[layer, "s"])
            far = lambda k: s.fst_in[layer, 3 + k]
            near = lambda k: s.fst_in[layer, k - 1]
            s.ds_out[:, block(core, 128)] = s.fst[layer, block(tp, 16), :] + near(2) + far(0) + far(2)
            s.ds_out[:, block(1 - core, 128)] = near(1) + near(3) + far(1) + far(3)

    small = {}

    def start_small(layer):
        mine = [links.plan(s.dp.at[layer], s.z_in.at[k - 1], links.along_tp(k), sec == layer) for k in (1, 2, 3)]
        theirs = [links.plan(s.dp.at[layer], s.z_in.at[3 + k], links.far_along_tp(k), sec != layer) for k in (0, 1, 2, 3)]
        theirs.append(links.plan(s.dt.at[layer], s.zt_in, links.other_section(), sec != layer))
        links.hold(mine + theirs)
        start_when(links, mine, sec == layer)
        start_when(links, theirs, sec != layer)
        small[layer] = mine + theirs

    def next_small(layer, n):
        when = sec == layer
        if n == 1:
            made = [links.plan(s.sp.at[0], s.sp_in.at[0, k - 1], links.along_y(k), when) for k in (1, 2, 3)]
            made += [
                links.plan(s.tp_sum.at[:, block((links.y + k) % side, 256)], s.ty_in.at[k - 1], links.along_y(k), when) for k in (1, 2, 3)
            ]
        elif n == 2:
            made = [links.plan(s.sp.at[1], s.sp_in.at[1, k - 1], links.along_x(k), when) for k in (1, 2, 3)]
            made += [
                links.plan(s.ty_sum.at[:, block((links.x + k) % side // 2, 128)], s.tx_in.at[k - 1], links.along_x(k), when) for k in (1, 2, 3)
            ]
        else:
            made = []
        links.hold(made)
        before = small[layer]

        @pl.when(when)
        def _():
            arrived(before)
            if n == 1:
                both = s.dp[layer] + s.z_in[3]
                shared = both
                for k in (0, 1, 2, 4, 5, 6):
                    shared = shared + s.z_in[k]
                row, lane = iota(both.shape, 0), iota(both.shape, 1)
                is_shared = (row == 6) | ((row < 5) & (lane >= inner) & (lane < inner + 256))
                s.sp[0] = jnp.where(is_shared, shared, both)
                s.tp_sum[...] = s.dt[layer] + s.zt_in[...]
            elif n == 2:
                s.sp[1] = s.sp[0] + s.sp_in[0, 0] + s.sp_in[0, 1] + s.sp_in[0, 2]
                s.ty_sum[...] = s.tp_sum[:, block(links.y, 256)] + s.ty_in[0] + s.ty_in[1] + s.ty_in[2]
            else:
                s.dp_out[...] = s.sp[1] + s.sp_in[1, 0] + s.sp_in[1, 1] + s.sp_in[1, 2]
                s.dt_out[...] = s.ty_sum[:, block(links.x // 2, 128)] + s.tx_in[0] + s.tx_in[1] + s.tx_in[2]
            links.begin(made)

        small[layer] = made

    work.start_back()
    arrived(moved[1, 0])
    work.middle(1, 0)
    work.gate_back(1, 0)
    stages[1, 0].cross()
    arrived(moved[1, 1])
    work.middle(1, 1)
    work.gate_back(1, 1)
    upper, lower = {}, {}
    stages[1, 1].cross()
    work.scan_back(1, 1)
    links.sent(stages[0, 0].pair + stages[0, 1].pair)
    work.normed_grad(1, 1, part[0])
    for j in (0, 1):
        stages[2, j] = RowStage(links, s, 2, j, part[0], s.e.at[0])
    stages[2, 1].start()
    weight_grads(1, ("z", "o"), upper)

    def upper_in(h, total):
        rows = slice(h * PIECE, (h + 1) * PIECE)
        grad = input_grad(total, s.res[0, rows, :].astype(BF16), s.cotangent[sec, rows, :], s.p[1, 6:7, :])
        s.grads[1, rows, :] = grad
        return grad.astype(BF16)

    def lower_in(h, total):
        rows = slice(h * PIECE, (h + 1) * PIECE)
        s.grads[0, rows, :] = input_grad(total, s.tokens[sec, rows, :], s.grads[1, rows, :].astype(BF16), s.p[0, 6:7, :])

    crosses = {}
    for j in (0, 1):
        crosses[j] = [
            links.plan(s.cross.at[:, own], s.cross.at[:, own], links.along_tp(k), links.far == j) for k in (1, 2, 3)
        ]
        links.hold(crosses[j])

    def send_cross(j):
        def run():
            product = s.grads[1].astype(BF16).astype(F32) * s.tot[...]
            s.cross[:, own] = exact_left(mm_nt, jnp.ones((8, product.shape[1]), BF16), product, 3)
            links.begin(crosses[j])

        return run

    def take_cross(j):
        for k in (1, 2, 3):
            when_arrived([crosses[j][k - 1]], (tp + 4 - k) % 4 // 2 == j)

    stages[2, 1].cross()
    work.scan_back(1, 0)
    stages[2, 1].total(upper_in, send_cross(1))
    work.normed_grad(1, 0, part[0])
    stages[2, 0].start()
    steps_of(upper, ("z", "o"))
    weight_grads(1, ("v0", "v1"), upper)
    stages[2, 0].cross()
    weight_grads(1, ("s",), upper)
    start_small(1)
    stages[2, 1].collect()

    work.start_back()
    take_cross(1)
    work.upstream(0, 1)
    steps_of(upper, ("z", "o"))
    start_state_sum(1, upper)
    work.gate_back(0, 1)
    stages[2, 0].total(upper_in, send_cross(0))
    steps_of(upper, ("v0", "v1"))
    work.scan_back(0, 1)
    steps_of(upper, ("s",))
    next_small(1, 1)
    links.sent(stages[1, 0].pair + stages[1, 1].pair)
    for j in (0, 1):
        stages[1, j].total(second_out)
    work.normed_grad(0, 1, part[1])
    for j in (0, 1):
        stages[3, j] = RowStage(links, s, 3, j, part[1])
    stages[3, 1].start()
    steps_of(upper, ("v0", "v1"))

    stages[2, 0].collect()
    take_cross(0)
    s.so_give[...] = jnp.where(sec == 0, s.res[1], s.res[0]).astype(BF16)
    so_move = links.send(s.so_give, s.so_take, links.other_section())
    work.upstream(0, 0)
    work.gate_back(0, 0)
    weight_grads(0, ("z", "o"), lower)
    stages[3, 1].cross()
    steps_of(upper, ("s",))
    end_sums(1, upper, ("z", "o"))
    next_small(1, 2)
    work.scan_back(0, 0)
    steps_of(lower, ("z", "o"))
    weight_grads(0, ("v0", "v1"), lower)
    weight_grads(0, ("s",), lower)
    work.normed_grad(0, 0, part[1])
    stages[3, 0].start()
    start_small(0)
    stages[3, 0].cross()
    stages[3, 1].total(lower_in)
    steps_of(lower, ("z", "o"))
    start_state_sum(0, lower)
    end_sums(1, upper, ("v0", "v1", "s"))
    steps_of(lower, ("v0", "v1"))
    next_small(1, 3)
    next_small(0, 1)
    stages[3, 0].total(lower_in)
    s.ig_give[...] = jnp.where(sec == 0, s.grads[1], s.grads[0]).astype(BF16)
    ig_move = links.send(s.ig_give, s.ig_take, links.other_section())
    end_state(1)
    end_sums(0, lower, ("z", "o"))
    steps_of(lower, ("s",))
    next_small(0, 2)
    steps_of(lower, ("v0", "v1", "s"))
    so_move.wait_recv()
    s.out[sec] = jnp.where(sec == 0, s.res[0], s.res[1])
    s.out[1 - sec] = s.so_take[...].astype(F32)
    s.inp[sec] = jnp.where(sec == 0, s.grads[0], s.grads[1])
    end_sums(0, lower, ("s", "v0", "v1"))
    next_small(0, 3)
    end_state(0)
    ig_move.wait_recv()
    s.inp[1 - sec] = s.ig_take[...].astype(F32)
    for layer in (1, 0):

        @pl.when(sec == layer)
        def _(layer=layer):
            arrived([across[layer, name] for name in ("z", "o", "v0", "v1")])
            s.dz_out[...] = s.fz[layer].astype(F32) + s.gz[layer].astype(F32)
            s.do_out[...] = s.fo[layer].astype(F32) + s.go[layer].astype(F32)
            for h in (0, 1):
                s.dv_out[:, 256 * h : 256 * (h + 1)] = s.fv[layer, h].astype(F32) + s.gv[layer, h].astype(F32)

    links.finish()


def finish_body(out, inp, dz, do, dv, dt, ds, dp,
                o_out, o_in, o_norm, o_gate, o_value, o_step, o_state, o_ck, o_co, o_sk, o_so, o_decay, o_bias, o_skip, o_mixer, o_outw):
    place = lax.axis_index("dp") * 4 + lax.axis_index("tp")
    inner = dz.shape[1]
    heads = o_decay.shape[1]
    o_out[0] = out[...]
    o_in[0] = inp[...]
    o_gate[0] = dz[...]
    o_value[0] = dv[...]
    depth = o_step.shape[2]
    tile = dt[...]
    o_step[0] = jnp.where(place // 4 % 2 == 0, tile, pltpu.roll(tile, 128 - depth, 1))[0:heads, 0:depth]
    o_state[0] = ds[...]
    width = dp.shape[1]
    count = o_norm.shape[1]
    o_norm[...] = pltpu.roll(dp[...], (width - count * place) % width, 1)[6:7, 0:count]
    shared = pltpu.roll(dp[:, inner : inner + 256], (256 - 4 * place) % 256, 1)
    o_sk[0] = shared[0:4, 0:4]
    o_so[...] = shared[4:5, 0:4]
    o_ck[0] = dp[0:4, 0:inner]
    o_co[...] = dp[4:5, 0:inner]
    o_mixer[...] = dp[5:6, 0:inner]
    o_decay[...] = dp[7:8, 0:heads]
    o_bias[...] = dp[7:8, 128 : 128 + heads]
    skip = jnp.broadcast_to(dp[7:8, 512:], (8, inner))
    o_skip[...] = exact(mm_nt, skip, spread_matrix(inner), 3)[0:1, 0:heads]
    o_outw[0] = do[...]


def shards(side, tokens, segments, cotangent, norm_gain, gate_weight, value_weight, step_weight, state_weight, conv_kernel, conv_offset,
           state_kernel, state_offset, decay_log, step_bias, skip_gain, mixer_gain, output_weight):
    own, width = tokens.shape[1:]
    rows = segments.shape[1]
    inner = conv_kernel.shape[2]
    depth = gate_weight.shape[1]
    heads = decay_log.shape[1]
    out_weight = output_weight[0].T
    step_weight = jnp.swapaxes(step_weight, 1, 2)
    ins = dict(tokens=tokens, segments=segments, cotangent=cotangent, norm_gain=norm_gain, gate_weight=gate_weight, value_weight=value_weight,
               step_weight=step_weight, state_weight=state_weight, conv_kernel=conv_kernel, conv_offset=conv_offset, state_kernel=state_kernel,
               state_offset=state_offset, decay_log=decay_log, step_bias=step_bias, skip_gain=skip_gain, mixer_gain=mixer_gain,
               out_weight=out_weight)
    outs = dict(
        out=(2, own, width), inp=(2, own, width), dz_out=(depth, inner), do_out=(depth, inner), dv_out=(depth, inner), dt_out=(8, 128),
        ds_out=(depth // 4, 256), dp_out=(8, width),
    )
    more = side - 1
    scratch = dict(
        p=((2, 8, width), F32), dp=((2, 8, width), F32), tiny=((8, 128), F32), seg=((rows + 16, 128), F32),
        rows=((2, rows, width), BF16), e=((2, rows, width), BF16),
        v=((2, rows + 8, inner), F32), bc=((2, rows + 8, 256), F32), q=((2, rows, 128), F32), z=((2, rows, inner), F32),
        y=((2, rows, inner), F32), kept=((2, rows // CHUNK, CHUNK, inner), BF16), state=((CHUNK, inner), F32), later=((8, inner + 256), F32),
        mixed=((rows, inner), BF16), dy=((rows, inner), F32), dproj=((rows, 2 * inner + 384), BF16),
        stat=((2, 8, rows), F32), stat_in=((2, 3, 8, rows), F32), mid=((2, 8, rows), F32), cross=((8, rows), F32),
        part=((2, rows, width), BF16), sib=((4, 2, own, width), BF16), chip=((4, 2, own, width), BF16),
        tot=((own, width), F32), res=((2, own, width), F32), grads=((2, own, width), F32),
        so_give=((own, width), BF16), so_take=((own, width), BF16), ig_give=((own, width), BF16), ig_take=((own, width), BF16),
        z_in=((7, 8, width), F32), zt_in=((8, width), F32), sp=((2, 8, width), F32), sp_in=((2, 3, 8, width), F32),
        tp_sum=((8, width), F32), ty_in=((3, 8, 256), F32), ty_sum=((8, 256), F32), tx_in=((3, 8, 128), F32), dt=((2, 8, width), F32),
        wt=((2, side, side, 8, 128), F32), wq=((2, 128, width), BF16), ds_pair=((2, side, side, depth, 128), BF16),
        fst=((2, depth, 128), F32), fst_in=((2, 7, depth // 4, 128), F32),
    )
    for key, parts, columns in (("z", (), inner), ("o", (), inner), ("v", (2,), inner // 2), ("s", (2,), 128)):
        scratch["w" + key] = ((2,) + parts + (side, side, depth, columns), BF16)
        scratch["d" + key] = ((2,) + parts + (side, side, depth, columns), BF16)
        if key != "s":
            scratch["f" + key] = ((2,) + parts + (depth, columns), BF16)
            scratch["g" + key] = ((2,) + parts + (depth, columns), BF16)
    for key, columns in (("z", inner), ("o", inner), ("v0", inner // 2), ("v1", inner // 2), ("s", 128)):
        scratch["a" + key] = ((2, 2, 2, depth, columns), BF16)
        scratch["b" + key] = ((2, 2, 2, 2, depth, columns), BF16)
        scratch["m" + key] = ((2, side, depth, columns), BF16)
        scratch["c" + key] = ((2, 3, depth, columns), BF16)
    vmem = pl.BlockSpec(memory_space=pltpu.VMEM)
    names = list(ins) + list(outs) + list(scratch) + ["send_sem", "recv_sem"]
    results = pl.pallas_call(
        functools.partial(relay_body, side, names),
        name="relay",
        out_shape=tuple(jax.ShapeDtypeStruct(dims, F32) for dims in outs.values()),
        in_specs=[vmem] * len(ins),
        out_specs=tuple(vmem for _ in outs),
        scratch_shapes=[pltpu.VMEM(*entry) for entry in scratch.values()] + [pltpu.SemaphoreType.DMA((SENDS,)), pltpu.SemaphoreType.DMA((COPIES,))],
        compiler_params=pltpu.CompilerParams(collective_id=1, has_side_effects=True, vmem_limit_bytes=VMEM_LIMIT),
    )(*ins.values())
    dims_out = (
        (1, 2, own, width), (1, 2, own, width), (1, width // 64), (1, depth, inner), (1, depth, inner), (1, heads, depth), (1, depth // 4, 256),
        (1, 4, inner), (1, inner), (1, 4, 4), (1, 4), (1, heads), (1, heads), (1, heads), (1, inner), (1, depth, inner),
    )
    final = pl.pallas_call(
        finish_body,
        name="finish",
        out_shape=tuple(jax.ShapeDtypeStruct(dims, F32) for dims in dims_out),
        in_specs=[vmem] * len(results),
        out_specs=tuple(vmem for _ in dims_out),
        compiler_params=pltpu.CompilerParams(vmem_limit_bytes=VMEM_LIMIT),
    )(*results)
    swapped = lambda i: jnp.swapaxes(final[i], 1, 2)
    return final[:5] + (swapped(5),) + final[6:15] + (swapped(15),)


def solution(mesh):
    in_specs = (
        P(None, ("dp", "tp"), None),
        P(None, "dp"),
        P(None, ("dp", "tp"), None),
        P("section", None),
        P("section", "dp", "tp"),
        P("section", "dp", "tp"),
        P("section", "dp", "tp"),
        P("section", "dp", None),
        P("section", None, "tp"),
        P("section", "tp"),
        P("section", None, None),
        P("section", None),
        P("section", "tp"),
        P("section", "tp"),
        P("section", "tp"),
        P("section", "tp"),
        P("section", "tp", "dp"),
    )
    out_specs = (
        P("section", None, ("dp", "tp"), None),
        P("section", None, ("dp", "tp"), None),
        P("section", ("dp", "tp")),
        P("section", "dp", "tp"),
        P("section", "dp", "tp"),
        P("section", "dp", "tp"),
        P("section", ("dp", "tp"), None),
        P("section", None, "tp"),
        P("section", "tp"),
        P("section", None, ("dp", "tp")),
        P("section", ("dp", "tp")),
        P("section", "tp"),
        P("section", "tp"),
        P("section", "tp"),
        P("section", "tp"),
        P("section", "tp", "dp"),
    )
    side = round(mesh.shape["dp"] ** 0.5)
    return jax.shard_map(functools.partial(shards, side), mesh=mesh, in_specs=in_specs, out_specs=out_specs, check_vma=False)
```
